256 devices in a mesh: region: 128 (over x, z, y), batch: 2 (over core).
Axes of the slice: x: 4, y: 4, z: 8, core: 2. Of those that a mesh axis runs over, the one named last changes fastest.
Arguments:
- child_pixels: int32 [256, 1024], P('region', 'batch'), may hold values from 0 to 255
- parent_pixels: int32 [128, 1024], P('region', 'batch'), may hold values from 0 to 255
- child_leaf: bfloat16 [256, 1024, 256], P('region'), may hold values from -9 to 310
- parent_leaf: bfloat16 [128, 1024, 256], P('region'), may hold values from -9 to 9
- edge_weights: bfloat16 [256, 1024, 1024], P('region'), may hold values from 1.3671875e-08 to 0.12890625
- parent_of: int32 [256], replicated, may hold values from 0 to 127, as said below
- parent_flows: bfloat16 [128, 1024, 1024], P('region', 'batch'), may hold values from 0.049804688 to 1
Outputs:
- parent_ll: float32 [128, 1024, 1024], P('region', 'batch')
- child_flows: bfloat16 [256, 1024, 1024], P('region', 'batch')
- new_weights: bfloat16 [256, 1024, 1024], P('region', 'batch')
The draws below stay inside these ranges and needn't reach their ends.
Inputs may be any that keep to these rules, and one draw needn't show every extreme that they name: `parent_of`: child c's parent is c // 2 - 1, c // 2 or c // 2 + 1.
All inputs are finite; a program needn't handle non-finite values.
Results may differ from the reference program's by a relative error of at most 0.012.
Values may be sent and summed in bfloat16 or wider, within the bound.
No kernel may reach another device: no remote copies, remote signals or barrier semaphores. Data moves between devices by JAX's collectives and lax.ppermute only.
A program may use at most 128 MiB of HBM per device.

```python
import math
import jax
import jax.numpy as jnp
from jax import lax

K = 1024
VALUES = 256
C_DEV = 2
SAMP_DEV = 512
CHILDREN = 256
PARENTS = 128
SAMPLES = 1024
N_BATCH = 2


def draw_child_leaf(key, part):
    first = jax.random.fold_in(key, 0)
    logits = jnp.clip(4.0 * jax.random.normal(first, (CHILDREN, K, VALUES), jnp.float32), -9.0, 9.0)
    return logits.astype(jnp.bfloat16)


def draw_edge_weights(key, part):
    logs = jnp.clip(2.5 * jax.random.normal(key, (CHILDREN, K, K), jnp.float32), -8.0, 8.0)
    return (jnp.exp(logs - 3.125) / K).astype(jnp.bfloat16)


def draw_parent_of(key, part):
    home = jnp.arange(CHILDREN, dtype=jnp.int32) // C_DEV
    moves = jax.random.randint(key, (CHILDREN,), -1, 2)
    parent = jnp.clip(home + moves, 0, PARENTS - 1)
    parent = parent.at[0].set(0).at[CHILDREN - 1].set(PARENTS - 1)
    return parent.astype(jnp.int32)


def place_ends(values, stream_key, low, top_value):
    index_at = [jax.random.randint(jax.random.fold_in(stream_key, axis), (), 0, length) for axis, length in enumerate(values.shape)]
    main_axis = values.shape.index(max(values.shape))
    next_to = index_at[:main_axis] + [(index_at[main_axis] + 1) % values.shape[main_axis]] + index_at[main_axis + 1:]
    return values.at[tuple(index_at)].set(low).at[tuple(next_to)].set(top_value)


def block_levels(rng, shape, cuts, low, top_value):
    factor_of, own = 1.0, jax.random.fold_in(rng, 6)
    for position, parts in cuts:
        heights = jnp.exp(jax.random.uniform(jax.random.fold_in(own, position), (parts,), jnp.float32, low / len(cuts), top_value / len(cuts)))
        factor_of = factor_of * jnp.repeat(heights, shape[position] // parts).reshape([-1 if axis == position else 1 for axis in range(len(shape))])
    return factor_of


def scatter_about(own_key, dims, width, limit, cuts=(), kind=jnp.bfloat16):
    drawn = width * jax.random.normal(own_key, dims, jnp.float32)
    if cuts:
        drawn = drawn * block_levels(own_key, dims, cuts, -0.22, 0.18)
    return jnp.clip(drawn, -limit, limit).astype(kind)


def setup_inputs(seed: int = 0) -> dict:
    arg_keys = jax.random.split(jax.random.key(seed), 8)
    child_pixels = place_ends(jax.random.randint(arg_keys[0], (CHILDREN, SAMPLES), 0, VALUES), jax.random.fold_in(arg_keys[0], 1), 0, VALUES - 1).astype(jnp.int32)
    parent_pixels = place_ends(jax.random.randint(arg_keys[1], (PARENTS, SAMPLES), 0, VALUES), jax.random.fold_in(arg_keys[1], 1), 0, VALUES - 1).astype(jnp.int32)
    child_leaf = draw_child_leaf(jax.random.fold_in(arg_keys[7], 71), 0)
    parent_leaf = scatter_about(arg_keys[3], (PARENTS, K, VALUES), 1.5, 9.0, ((0, 128),))
    edge_weights = draw_edge_weights(jax.random.fold_in(arg_keys[7], 71), 0)
    parent_of = draw_parent_of(jax.random.fold_in(arg_keys[7], 71), 0)
    parent_flows = jnp.clip(jnp.exp(math.log(1.0) - 2.9996462 * jax.random.uniform(arg_keys[6], (PARENTS, SAMPLES, K), jnp.float32) ** block_levels(arg_keys[6], (PARENTS, SAMPLES, K), ((0, 128), (1, 2)), -0.2, 0.2)), 0.049804688, 1.0).astype(jnp.bfloat16)
    return dict(child_pixels=child_pixels, parent_pixels=parent_pixels, child_leaf=child_leaf, parent_leaf=parent_leaf, edge_weights=edge_weights, parent_of=parent_of, parent_flows=parent_flows)


PRIOR = 0.05


def leaf_rows(leaf, pixels):
    table = jax.nn.log_softmax(leaf.astype(jnp.float32), axis=-1)
    return jnp.transpose(table)[pixels]


def parent_rows(inputs):
    return leaf_rows(inputs[0], inputs[1])


def reference(child_pixels, parent_pixels, child_leaf, parent_leaf, edge_weights, parent_of, parent_flows):
    start = lax.map(parent_rows, (parent_leaf, parent_pixels))

    def child_step(carry, inputs):
        leaf, pixels, weights, parent = inputs
        loglik = leaf_rows(leaf, pixels)
        row_peak = jnp.max(loglik, axis=-1, keepdims=True)
        shifted = jnp.exp(loglik - row_peak).astype(jnp.bfloat16)
        shifted_wide = shifted.astype(jnp.float32)
        dense = weights.astype(jnp.float32)
        totals = jnp.dot(shifted_wide, dense.T, precision=lax.Precision.HIGHEST)
        message = row_peak + jnp.log(totals)
        carry = carry.at[parent].add(message)
        upstream = parent_flows[parent].astype(jnp.float32)
        scaled = (upstream / totals).astype(jnp.bfloat16)
        scaled_wide = scaled.astype(jnp.float32)
        pulled = jnp.dot(scaled_wide, dense, precision=lax.Precision.HIGHEST)
        flows = (shifted_wide * pulled).astype(jnp.bfloat16)
        halves_a = scaled_wide.reshape(N_BATCH, SAMP_DEV, K)
        halves_e = shifted_wide.reshape(N_BATCH, SAMP_DEV, K)
        partial_value = jnp.einsum("hbk,hbj->hkj", halves_a, halves_e, precision=lax.Precision.HIGHEST)
        partial_value = lax.optimization_barrier(partial_value.astype(jnp.bfloat16)).astype(jnp.float32)
        summed = jnp.sum(partial_value, axis=0)
        counts = dense * summed + PRIOR
        fresh = (K * counts / jnp.sum(counts, axis=-1, keepdims=True)).astype(jnp.bfloat16)
        return carry, (flows, fresh)

    parent_ll, outputs = lax.scan(child_step, start, (child_leaf, child_pixels, edge_weights, parent_of))
    return parent_ll, outputs[0], outputs[1]
```

```python
import functools

import jax
import jax.numpy as jnp
from jax import lax
from jax.experimental import pallas as pl
from jax.experimental.pallas import tpu as pltpu
from jax.sharding import PartitionSpec as P

PRIOR = 0.05
F32, BF16 = jnp.float32, jnp.bfloat16
MIB = 2**20


def log_softmax_by_value(leaf):
    logits = jnp.transpose(leaf.astype(F32))
    top = jnp.max(logits, axis=0, keepdims=True)
    logits = logits - top
    return logits - jnp.log(jnp.sum(jnp.exp(logits), axis=0, keepdims=True))


def one_hot_rows(pixels, values):
    rows = lax.broadcasted_iota(jnp.int32, (values, pixels.shape[1]), 0)
    return jnp.where(rows == pixels, 1.0, 0.0).astype(F32)


def params(limit):
    return pltpu.CompilerParams(vmem_limit_bytes=limit * MIB)


def cost(flops, moved, exps=0):
    return pl.CostEstimate(flops=flops, bytes_accessed=moved, transcendentals=exps)


def tables_kernel(
    ids_ref, leaf_ref, weights_ref, mine_ref, theirs_ref, shifted_ref, inverse_ref, message_ref, sent_ref
):
    child = pl.program_id(0)
    table = log_softmax_by_value(leaf_ref[0])
    peak = jnp.max(table, axis=1, keepdims=True)
    shifted = jnp.exp(table - peak).astype(BF16)
    shifted_ref[0] = shifted
    totals = lax.dot_general(
        shifted, weights_ref[0], (((1,), (1,)), ((), ())), preferred_element_type=F32
    )
    inverse_ref[0] = (1.0 / totals).astype(BF16)
    message = (peak + jnp.log(totals)).astype(BF16)
    message_ref[0] = message
    values = message.shape[0]
    start = pl.multiple_of(child * values, values)
    sent_ref[pl.ds(start, values)] = message

    @pl.when(child == 0)
    def _():
        core = ids_ref[ids_ref.shape[0] - 1]
        own = jnp.concatenate([mine_ref[c] for c in range(mine_ref.shape[0])], axis=1)
        other = jnp.concatenate([theirs_ref[c] for c in range(mine_ref.shape[0])], axis=1)
        half = lax.broadcasted_iota(jnp.int32, (16, own.shape[1]), 0)
        rows = jnp.where(half == core, own, other).astype(F32).astype(BF16)
        sent_ref[sent_ref.shape[0] - 16 :] = rows


def tables(ids, leaf, weights, mine, theirs):
    children, states, values = leaf.shape
    one = lambda *block: pl.BlockSpec((1, *block), lambda c, ids: (c, 0, 0))
    pixels = pl.BlockSpec(mine.shape, lambda c, ids: (0, 0, 0))
    rows = children * values + 16
    return pl.pallas_call(
        tables_kernel,
        grid_spec=pltpu.PrefetchScalarGridSpec(
            num_scalar_prefetch=1,
            grid=(children,),
            in_specs=[one(states, values), one(states, states), pixels, pixels],
            out_specs=[one(values, states)] * 3
            + [pl.BlockSpec((rows, states), lambda c, ids: (0, 0))],
        ),
        out_shape=[jax.ShapeDtypeStruct((children, values, states), BF16)] * 3
        + [jax.ShapeDtypeStruct((rows, states), BF16)],
        compiler_params=params(60),
        cost_estimate=cost(2 * children * values * states**2, 12 * MIB),
        name="tables",
    )(ids, leaf, weights, mine, theirs)


def after(value, *others):
    anywhere = pl.BlockSpec(memory_space=pl.ANY)
    return pl.pallas_call(
        lambda *refs: None,
        in_specs=[anywhere] * (1 + len(others)),
        out_specs=anywhere,
        out_shape=jax.ShapeDtypeStruct(value.shape, value.dtype),
        input_output_aliases={0: 0},
        compiler_params=params(60),
        cost_estimate=cost(0, 0),
        name="after",
    )(value, *others)


def home_kernel(ids_ref, parent_pix_ref, child_pix_ref, leaf_ref, message_ref, out_ref):
    position = ids_ref[ids_ref.shape[0] - 2]
    children, values, _ = message_ref.shape
    logits = leaf_ref[0]
    wide = logits.astype(F32)
    top = jnp.max(wide, axis=1, keepdims=True)
    norm = top + jnp.log(jnp.sum(jnp.exp(wide - top), axis=1, keepdims=True))
    norm_row = jnp.transpose(jnp.broadcast_to(norm, (norm.shape[0], 128)))[:1]
    hot = jnp.transpose(one_hot_rows(parent_pix_ref[0], values)).astype(BF16)
    total = (
        lax.dot_general(hot, logits, (((1,), (1,)), ((), ())), preferred_element_type=F32)
        - norm_row
    )
    for c in range(children):
        mine = jnp.where(ids_ref[position * children + c] == position, 1.0, 0.0)
        hot = jnp.transpose(one_hot_rows(child_pix_ref[c], values) * mine).astype(BF16)
        total = total + jnp.dot(hot, message_ref[c], preferred_element_type=F32)
    out_ref[0] = total


def home(ids, parent_pix, child_pix, leaf, message):
    children, values, states = message.shape
    samples = parent_pix.shape[2]
    whole = lambda shape: pl.BlockSpec(shape, lambda i, ids: (0,) * len(shape))
    return pl.pallas_call(
        home_kernel,
        grid_spec=pltpu.PrefetchScalarGridSpec(
            num_scalar_prefetch=1,
            grid=(1,),
            in_specs=[whole(a.shape) for a in (parent_pix, child_pix, leaf, message)],
            out_specs=whole((1, samples, states)),
        ),
        out_shape=jax.ShapeDtypeStruct((1, samples, states), F32),
        compiler_params=params(60),
        cost_estimate=cost(6 * samples * states * values, 4 * MIB),
        name="home",
    )(ids, parent_pix, child_pix, leaf, message)


def flows_kernel(
    ids_ref, pix_ref, before_ref, here_ref, after_ref, shifted_ref, inverse_ref, weights_ref,
    flows_ref, sums_ref,
):
    child, part = pl.program_id(0), pl.program_id(1)
    position = ids_ref[ids_ref.shape[0] - 2]
    source = ids_ref[position * pl.num_programs(0) + child] - position
    above = jnp.where(
        source == 0, here_ref[0], jnp.where(source < 0, before_ref[0], after_ref[0])
    )
    values = shifted_ref.shape[1]
    hot_rows = one_hot_rows(pix_ref[0], values)
    hot = jnp.transpose(hot_rows).astype(BF16)
    inverse = jnp.dot(hot, inverse_ref[0], preferred_element_type=F32)
    scaled = (above.astype(F32) * inverse).astype(BF16)
    pulled = jnp.dot(scaled, weights_ref[0], preferred_element_type=F32)
    shifted = jnp.dot(hot, shifted_ref[0], preferred_element_type=F32)
    flows_ref[0] = (shifted * pulled).astype(BF16)
    sums = jnp.dot(hot_rows.astype(BF16), above, preferred_element_type=F32)

    @pl.when(part == 0)
    def _():
        sums_ref[0] = sums

    @pl.when(part > 0)
    def _():
        sums_ref[0] += sums


def flows(ids, pix, before, here, after, shifted, inverse, weights):
    children, values, states = shifted.shape
    samples = here.shape[1]
    rows = samples // 2
    near = pl.BlockSpec((1, rows, states), lambda c, i, ids: (0, i, 0))
    one = lambda *block: pl.BlockSpec((1, *block), lambda c, i, ids: (c, 0, 0))
    return pl.pallas_call(
        flows_kernel,
        grid_spec=pltpu.PrefetchScalarGridSpec(
            num_scalar_prefetch=1,
            grid=(children, samples // rows),
            in_specs=[
                pl.BlockSpec((1, 1, rows), lambda c, i, ids: (c, 0, i)),
                near,
                near,
                near,
                one(values, states),
                one(values, states),
                one(states, states),
            ],
            out_specs=[
                pl.BlockSpec((1, rows, states), lambda c, i, ids: (c, i, 0)),
                one(values, states),
            ],
        ),
        out_shape=[
            jax.ShapeDtypeStruct((children, samples, states), BF16),
            jax.ShapeDtypeStruct((children, values, states), F32),
        ],
        compiler_params=params(60),
        cost_estimate=cost(2 * children * samples * states * (states + 3 * values), 12 * MIB),
        name="flows",
    )(ids, pix, before, here, after, shifted, inverse, weights)


def update_kernel(ids_ref, mine_ref, theirs_ref, inverse_ref, shifted_ref, weights_ref, out_ref):
    sums = (mine_ref[0] + theirs_ref[0].astype(F32)) * inverse_ref[0].astype(F32)
    pairs = jnp.dot(
        jnp.transpose(sums).astype(BF16), shifted_ref[0], preferred_element_type=F32
    )
    counts = weights_ref[0].astype(F32) * pairs + PRIOR
    scale = counts.shape[1] / jnp.sum(counts, axis=1, keepdims=True)
    out_ref[0] = (counts * scale).astype(BF16)


def update(ids, sums, theirs, inverse, shifted, weights):
    children, values, states = shifted.shape
    rows = theirs.shape[2]
    core = ids.shape[0] - 1
    return pl.pallas_call(
        update_kernel,
        grid_spec=pltpu.PrefetchScalarGridSpec(
            num_scalar_prefetch=1,
            grid=(children,),
            in_specs=[
                pl.BlockSpec((1, values, rows), lambda c, ids: (c, 0, ids[core])),
                pl.BlockSpec((1, values, rows), lambda c, ids: (c, 0, 0)),
                pl.BlockSpec((1, values, rows), lambda c, ids: (c, 0, ids[core])),
                pl.BlockSpec((1, values, states), lambda c, ids: (c, 0, 0)),
                pl.BlockSpec((1, rows, states), lambda c, ids: (c, ids[core], 0)),
            ],
            out_specs=pl.BlockSpec((1, rows, states), lambda c, ids: (c, 0, 0)),
        ),
        out_shape=jax.ShapeDtypeStruct((children, rows, states), BF16),
        compiler_params=params(60),
        cost_estimate=cost(2 * children * rows * states * values, 8 * MIB),
        name="update",
    )(ids, sums, theirs, inverse, shifted, weights)


def gather_kernel(children, ids_ref, landed_ref, other_ref, sofar_ref, out_ref):
    count = ids_ref.shape[0] - 2
    position, core = ids_ref[count], ids_ref[count + 1]
    samples = out_ref.shape[1]
    values = (landed_ref.shape[0] - 16) // children
    total = sofar_ref[0]
    for table_ref, from_low in ((landed_ref, core == 0), (other_ref, core == 1)):
        halves = table_ref[children * values :].astype(F32)
        pixels = jnp.where(core == 0, halves[0:1], halves[1:2]).astype(jnp.int32)
        neighbour = jnp.where(from_low, position - 1, position + 1)
        for c in range(children):
            child = neighbour * children + c
            there = jnp.logical_and(child >= 0, child < count)
            parent = ids_ref[jnp.clip(child, 0, count - 1)]
            mine = jnp.where(jnp.logical_and(there, parent == position), 1.0, 0.0)
            hot = one_hot_rows(pixels[:, c * samples : (c + 1) * samples], values)
            hot = jnp.transpose(hot * mine).astype(BF16)
            table = table_ref[c * values : (c + 1) * values]
            total = total + jnp.dot(hot, table, preferred_element_type=F32)
    out_ref[0] = total


def gather(children, ids, landed, other, sofar):
    whole = lambda shape: pl.BlockSpec(shape, lambda i, ids: (0,) * len(shape))
    return pl.pallas_call(
        functools.partial(gather_kernel, children),
        grid_spec=pltpu.PrefetchScalarGridSpec(
            num_scalar_prefetch=1,
            grid=(1,),
            in_specs=[whole(a.shape) for a in (landed, other, sofar)],
            out_specs=whole(sofar.shape),
        ),
        out_shape=jax.ShapeDtypeStruct(sofar.shape, F32),
        input_output_aliases={3: 0},
        compiler_params=params(60),
        cost_estimate=cost(2 * sofar.shape[1] * landed.shape[0] * landed.shape[1], 6 * MIB),
        name="gather",
    )(ids, landed, other, sofar)


def on_device(
    child_pixels, parent_pixels, child_leaf, parent_leaf, edge_weights, parent_of, parent_flows
):
    regions, cores = lax.axis_size("region"), lax.axis_size("batch")
    position, core = lax.axis_index("region"), lax.axis_index("batch")
    up = [(i, i + 1) for i in range(regions - 1)]
    down = [(i + 1, i) for i in range(regions - 1)]
    swap = [(0, 1), (1, 0)]
    children, samples = child_pixels.shape
    states = edge_weights.shape[1]
    ids = jnp.concatenate([parent_of, jnp.stack([position, core]).astype(jnp.int32)])
    child_pix = child_pixels[:, None, :]
    low = lax.ppermute(parent_flows, "region", up)
    high = lax.ppermute(parent_flows, "region", down)
    other_pix = lax.ppermute(child_pixels, "batch", swap)[:, None, :]
    shifted, inverse, message, sent = tables(ids, child_leaf, edge_weights, child_pix, other_pix)
    near = home(ids, parent_pixels[:, None, :], child_pix, parent_leaf, message)
    pairs = [(cores * i, cores * j) for i, j in up] + [(cores * i + 1, cores * j + 1) for i, j in down]
    landed = lax.ppermute(after(sent, low, high, near), ("region", "batch"), pairs)
    child_flows, sums = flows(
        ids, child_pix, low, parent_flows, high, shifted, inverse, edge_weights
    )
    own_rows = states // cores
    outgoing = lax.dynamic_slice_in_dim(sums, (1 - core) * own_rows, own_rows, 2).astype(BF16)
    theirs = lax.ppermute(outgoing, "batch", swap)
    other = lax.ppermute(after(landed, theirs), "batch", swap)
    new_weights = update(ids, sums, theirs, inverse, shifted, edge_weights)
    parent_ll = gather(children, ids, landed, other, near)
    return parent_ll, child_flows, new_weights


def solution(mesh):
    return jax.shard_map(
        on_device,
        mesh=mesh,
        in_specs=(
            P("region", "batch"),
            P("region", "batch"),
            P("region", None, None),
            P("region", None, None),
            P("region", None, None),
            P(),
            P("region", "batch", None),
        ),
        out_specs=(
            P("region", "batch", None),
            P("region", "batch", None),
            P("region", "batch", None),
        ),
        check_vma=False,
    )
```

```python
import functools

import jax
import jax.numpy as jnp
from jax import lax
from jax.experimental import pallas as pl
from jax.experimental.pallas import tpu as pltpu
from jax.sharding import PartitionSpec as P

PRIOR = 0.05
F32, BF16 = jnp.float32, jnp.bfloat16
MIB = 2**20


def log_softmax_by_value(leaf):
    logits = jnp.transpose(leaf.astype(F32))
    top = jnp.max(logits, axis=0, keepdims=True)
    logits = logits - top
    return logits - jnp.log(jnp.sum(jnp.exp(logits), axis=0, keepdims=True))


def one_hot_rows(pixels, values):
    rows = lax.broadcasted_iota(jnp.int32, (values, pixels.shape[1]), 0)
    return jnp.where(rows == pixels, 1.0, 0.0).astype(F32)


def one_hot(pixels, values):
    count = pixels.shape[1]
    column = jnp.transpose(jnp.broadcast_to(pixels.astype(F32), (8, count)))[:, :1]
    columns = lax.broadcasted_iota(jnp.int32, (count, values), 1).astype(F32)
    return jnp.where(columns == column, 1.0, 0.0).astype(BF16)


def dot(a, b):
    return jnp.dot(a, b, preferred_element_type=F32)


def dot_t(a, b):
    return lax.dot_general(a, b, (((1,), (1,)), ((), ())), preferred_element_type=F32)


def call(kernel, name, grid, in_specs, out_specs, out_shape, args, flops, scalars=1, vmem=26, **more):
    return pl.pallas_call(
        kernel,
        grid_spec=pltpu.PrefetchScalarGridSpec(
            num_scalar_prefetch=scalars,
            grid=grid,
            in_specs=in_specs,
            out_specs=out_specs,
            scratch_shapes=more.pop("scratch", ()),
        ),
        out_shape=out_shape,
        compiler_params=pltpu.CompilerParams(vmem_limit_bytes=vmem * MIB),
        cost_estimate=pl.CostEstimate(flops=flops // 10**6, bytes_accessed=8, transcendentals=0),
        name=name,
        **more,
    )(*args)


def shape(*dims, dtype=BF16):
    return jax.ShapeDtypeStruct(dims, dtype)


TOKEN = shape(8, 128, dtype=F32)


def whole(array):
    return pl.BlockSpec(array.shape, lambda *_: (0,) * array.ndim)


def after(value, *others):
    anywhere = pl.BlockSpec(memory_space=pl.ANY)
    return pl.pallas_call(
        lambda *refs: None,
        in_specs=[anywhere] * (1 + len(others)),
        out_specs=anywhere,
        out_shape=jax.ShapeDtypeStruct(value.shape, value.dtype),
        input_output_aliases={0: 0},
        compiler_params=pltpu.CompilerParams(vmem_limit_bytes=MIB),
        cost_estimate=pl.CostEstimate(flops=0, bytes_accessed=0, transcendentals=0),
        name="after",
    )(value, *others)


def tables_kernel(
    leaf_ref, weights_ref, mine_ref, theirs_ref, shifted_ref, inverse_ref, message_ref, sent_ref
):
    child = pl.program_id(0)
    table = log_softmax_by_value(leaf_ref[0])
    peak = jnp.max(table, axis=1, keepdims=True)
    shifted = jnp.exp(table - peak).astype(BF16)
    shifted_ref[0] = shifted
    totals = dot_t(shifted, weights_ref[0])
    inverse_ref[0] = (1.0 / totals).astype(BF16)
    message = (peak + jnp.log(totals)).astype(BF16)
    message_ref[0] = message
    values = message.shape[0]
    sent_ref[pl.ds(pl.multiple_of(child * values, values), values)] = message

    @pl.when(child == 0)
    def _():
        children = mine_ref.shape[0]
        own = jnp.concatenate([mine_ref[c : c + 1] for c in range(children)], axis=1)
        other = jnp.concatenate([theirs_ref[c : c + 1] for c in range(children)], axis=1)
        half = lax.broadcasted_iota(jnp.int32, (16, own.shape[1]), 0)
        rows = jnp.where(half == lax.axis_index("batch"), own, other)
        sent_ref[sent_ref.shape[0] - 16 :] = rows.astype(F32).astype(BF16)


def tables(leaf, weights, mine, theirs):
    children, states, values = leaf.shape
    one = lambda *block: pl.BlockSpec((1, *block), lambda c: (c, 0, 0))
    sent = shape(children * values + 16, states)
    return call(
        tables_kernel, "tables", (children,),
        [one(states, values), one(states, states), whole(mine), whole(theirs)],
        [one(values, states)] * 3 + [whole(sent)],
        [shape(children, values, states)] * 3 + [sent],
        (leaf, weights, mine, theirs),
        2 * children * values * states**2,
        scalars=0,
    )


def rows_kernel(
    ids_ref, parent_pix_ref, pix_ref, leaf_ref, message_ref, shifted_ref, inverse_ref,
    shifted_rows_ref, inverse_rows_ref, out_ref, token_ref,
):
    token_ref[...] = jnp.zeros_like(token_ref)
    child, children = pl.program_id(0), pix_ref.shape[0]
    position = lax.axis_index("region")
    values = message_ref.shape[1]
    hot = one_hot(pix_ref[pl.ds(child, 1)], values)
    shifted_rows_ref[0] = dot(hot, shifted_ref[0]).astype(BF16)
    inverse_rows_ref[0] = dot(hot, inverse_ref[0]).astype(BF16)
    mine = jnp.where(ids_ref[position * children + child] == position, 1.0, 0.0)
    message = dot(hot, message_ref[0]) * mine

    @pl.when(child == 0)
    def _():
        logits = leaf_ref[0]
        wide = logits.astype(F32)
        top = jnp.max(wide, axis=1, keepdims=True)
        norm = top + jnp.log(jnp.sum(jnp.exp(wide - top), axis=1, keepdims=True))
        norm_row = jnp.transpose(jnp.broadcast_to(norm, (norm.shape[0], 128)))[:1]
        parent_hot = one_hot(parent_pix_ref[...], values)
        out_ref[0] = dot_t(parent_hot, logits) - norm_row + message

    @pl.when(child > 0)
    def _():
        out_ref[0] += message


def rows(ids, parent_pix, pix, leaf, message, shifted, inverse):
    children, values, states = message.shape
    samples = pix.shape[1]
    one = lambda *block: pl.BlockSpec((1, *block), lambda c, ids: (c, 0, 0))
    out = shape(1, samples, states, dtype=F32)
    return call(
        rows_kernel, "rows", (children,),
        [whole(parent_pix), whole(pix), whole(leaf)] + [one(values, states)] * 3,
        [one(samples, states)] * 2 + [whole(out), whole(TOKEN)],
        [shape(children, samples, states)] * 2 + [out, TOKEN],
        (ids, parent_pix, pix, leaf, message, shifted, inverse),
        2 * samples * states * values * (3 * children + 1),
    )


def flows_kernel(
    ids_ref, pix_ref, before_ref, here_ref, after_ref, shifted_ref, inverse_ref, weights_ref,
    flows_ref, mine_ref, theirs_ref,
):
    child, children = pl.program_id(0), pl.num_programs(0)
    position, core = lax.axis_index("region"), lax.axis_index("batch")
    source = ids_ref[position * children + child] - position
    above = jnp.where(
        source == 0, here_ref[0], jnp.where(source < 0, before_ref[0], after_ref[0])
    )
    scaled = (above.astype(F32) * inverse_ref[0].astype(F32)).astype(BF16)
    pulled = dot(scaled, weights_ref[0])
    flows_ref[0] = (shifted_ref[0].astype(F32) * pulled).astype(BF16)
    values, part = mine_ref.shape[1:]
    hot_rows = one_hot_rows(pix_ref[pl.ds(child, 1)], values).astype(BF16)
    sums = dot(hot_rows, above)
    low, high = sums[:, :part], sums[:, part:]
    mine_ref[0] = jnp.where(core == 0, low, high)
    theirs_ref[0] = jnp.where(core == 0, high, low).astype(BF16)


def flows(ids, pix, before, here, after, shifted, inverse, weights, values):
    children, samples, states = shifted.shape
    one = lambda *block: pl.BlockSpec((1, *block), lambda c, ids: (c, 0, 0))
    return call(
        flows_kernel, "flows", (children,),
        [whole(pix), whole(before), whole(here), whole(after)]
        + [one(samples, states)] * 2 + [one(states, states)],
        [one(samples, states), one(values, states // 2), one(values, states // 2)],
        [
            shape(children, samples, states),
            shape(children, values, states // 2, dtype=F32),
            shape(children, values, states // 2),
        ],
        (ids, pix, before, here, after, shifted, inverse, weights),
        5 * 10**16,
        vmem=26,
    )


def update_kernel(
    mine_ref, theirs_ref, inverse_ref, shifted_ref, weights_ref, out_ref, token_ref, held_ref, sems
):
    child, step = pl.program_id(0), pl.program_id(1)
    children, count, _ = held_ref.shape
    width = out_ref.shape[1]
    start = pl.multiple_of(lax.axis_index("batch") * count, count)
    token_ref[...] = jnp.zeros_like(token_ref)

    def fetch(c):
        return pltpu.make_async_copy(
            weights_ref.at[c, pl.ds(start, count)], held_ref.at[c], sems.at[c]
        )

    @pl.when(jnp.logical_and(child == 0, step == 0))
    def _():
        for c in range(children):
            fetch(c).start()

    here = pl.multiple_of(step * width, width)
    inverse = inverse_ref[0, :, pl.ds(pl.multiple_of(start + here, width), width)]
    sums = (mine_ref[0] + theirs_ref[0].astype(F32)) * inverse.astype(F32)
    pairs = dot(jnp.transpose(sums).astype(BF16), shifted_ref[0])

    @pl.when(step == 0)
    def _():
        fetch(child).wait()

    counts = held_ref[child, pl.ds(here, width)].astype(F32) * pairs + PRIOR
    scale = counts.shape[1] / jnp.sum(counts, axis=1, keepdims=True)
    out_ref[0] = (counts * scale).astype(BF16)


def update(mine, theirs, inverse, shifted, weights):
    children, values, states = shifted.shape
    count = mine.shape[2]
    steps = 2
    width = count // steps
    block = pl.BlockSpec((1, values, width), lambda c, i: (c, 0, i))
    table = pl.BlockSpec((1, values, states), lambda c, i: (c, 0, 0))
    return call(
        update_kernel, "update", (children, steps),
        [block, block, table, table, pl.BlockSpec(memory_space=pltpu.HBM)],
        [pl.BlockSpec((1, width, states), lambda c, i: (c, i, 0)), whole(TOKEN)],
        [shape(children, count, states), TOKEN],
        (mine, theirs, inverse, shifted, weights),
        2 * children * count * states * values,
        vmem=26,
        scalars=0,
        scratch=[pltpu.VMEM((children, count, states), BF16), pltpu.SemaphoreType.DMA((children,))],
    )


def gather_kernel(children, landed, ids_ref, table_ref, pix_ref, sofar_ref, out_ref, hot_ref):
    count = ids_ref.shape[0]
    position, core = lax.axis_index("region"), lax.axis_index("batch")
    samples = out_ref.shape[1]
    values = table_ref.shape[0] // children
    neighbour = jnp.where((core == 0) == landed, position - 1, position + 1)
    out_ref[...] = sofar_ref[...]
    for c in range(children):
        child = neighbour * children + c
        there = jnp.logical_and(child >= 0, child < count)
        parent = ids_ref[jnp.clip(child, 0, count - 1)]

        @pl.when(jnp.logical_and(there, parent == position))
        def _():
            @pl.when(pl.program_id(0) == 0)
            def _():
                halves = pix_ref[...].astype(F32)
                pixels = jnp.where(core == 0, halves[0:1], halves[1:2])
                hot_ref[c] = one_hot(pixels[:, c * samples : (c + 1) * samples], values)

            out_ref[0] += dot(hot_ref[c], table_ref[c * values : (c + 1) * values])


def gather(children, landed, ids, tables, sofar):
    samples, states = sofar.shape[1:]
    span = tables.shape[0] - 16
    steps = 4
    width = states // steps
    out = pl.BlockSpec((1, samples, width), lambda i, ids: (0, 0, i))
    return call(
        functools.partial(gather_kernel, children, landed), "landed" if landed else "other", (steps,),
        [
            pl.BlockSpec((span, width), lambda i, ids: (0, i)),
            pl.BlockSpec((16, states), lambda i, ids: (span // 16, 0)),
            out,
        ],
        out, shape(*sofar.shape, dtype=F32),
        (ids, tables, tables, sofar),
        2 * samples * span * states,
        vmem=20,
        scratch=[pltpu.VMEM((children, samples, span // children), BF16)],
    )


def on_device(
    child_pixels, parent_pixels, child_leaf, parent_leaf, edge_weights, parent_of, parent_flows
):
    regions, cores = lax.axis_size("region"), lax.axis_size("batch")
    up = [(i, i + 1) for i in range(regions - 1)]
    down = [(i + 1, i) for i in range(regions - 1)]
    swap = [(0, 1), (1, 0)]
    children, values = child_pixels.shape[0], child_leaf.shape[2]

    low = lax.ppermute(parent_flows, "region", up)
    high = lax.ppermute(parent_flows, "region", down)
    other_pix = lax.ppermute(child_pixels, "batch", swap)
    shifted, inverse, message, sent = tables(child_leaf, edge_weights, child_pixels, other_pix)
    shifted_rows, inverse_rows, near, looked_up = rows(
        parent_of, parent_pixels, child_pixels, parent_leaf, message, shifted, inverse
    )
    pairs = [(cores * i, cores * j) for i, j in up] + [(cores * i + 1, cores * j + 1) for i, j in down]
    landed = lax.ppermute(after(sent, looked_up), ("region", "batch"), pairs)
    child_flows, mine, theirs = flows(
        parent_of, child_pixels, low, parent_flows, high, shifted_rows, inverse_rows, edge_weights, values
    )
    theirs = lax.ppermute(theirs, "batch", swap)
    new_weights, updated = update(mine, theirs, inverse, shifted, edge_weights)
    landed = after(landed, updated)
    other = lax.ppermute(landed, "batch", swap)
    near = gather(children, True, parent_of, landed, near)
    parent_ll = gather(children, False, parent_of, other, near)
    return parent_ll, child_flows, new_weights


def solution(mesh):
    return jax.shard_map(
        on_device,
        mesh=mesh,
        in_specs=(
            P("region", "batch"),
            P("region", "batch"),
            P("region", None, None),
            P("region", None, None),
            P("region", None, None),
            P(),
            P("region", "batch", None),
        ),
        out_specs=(
            P("region", "batch", None),
            P("region", "batch", None),
            P("region", "batch", None),
        ),
        check_vma=False,
    )
```

```python
import functools

import jax
import jax.numpy as jnp
from jax import lax
from jax.experimental import pallas as pl
from jax.experimental.pallas import tpu as pltpu
from jax.sharding import PartitionSpec as P

PRIOR = 0.05
STRIP = 128
F32, BF16 = jnp.float32, jnp.bfloat16
MIB = 2**20


def log_softmax_by_value(leaf):
    logits = jnp.transpose(leaf.astype(F32))
    top = jnp.max(logits, axis=0, keepdims=True)
    logits = logits - top
    return logits - jnp.log(jnp.sum(jnp.exp(logits), axis=0, keepdims=True))


def one_hot_rows(pixels, values):
    rows = lax.broadcasted_iota(jnp.int32, (values, pixels.shape[1]), 0)
    return jnp.where(rows == pixels, 1.0, 0.0).astype(F32)


def one_hot(pixels, values):
    count = pixels.shape[1]
    column = jnp.transpose(jnp.broadcast_to(pixels.astype(F32), (8, count)))[:, :1]
    columns = lax.broadcasted_iota(jnp.int32, (count, values), 1).astype(F32)
    return jnp.where(columns == column, 1.0, 0.0).astype(BF16)


def dot(a, b):
    return jnp.dot(a, b, preferred_element_type=F32)


def dot_t(a, b):
    return lax.dot_general(a, b, (((1,), (1,)), ((), ())), preferred_element_type=F32)


def call(kernel, name, grid, in_specs, out_specs, out_shape, args, flops, scalars=1, vmem=26, **more):
    return pl.pallas_call(
        kernel,
        grid_spec=pltpu.PrefetchScalarGridSpec(
            num_scalar_prefetch=scalars,
            grid=grid,
            in_specs=in_specs,
            out_specs=out_specs,
            scratch_shapes=more.pop("scratch", ()),
        ),
        out_shape=out_shape,
        compiler_params=pltpu.CompilerParams(vmem_limit_bytes=vmem * MIB),
        cost_estimate=pl.CostEstimate(flops=flops // 10**6, bytes_accessed=8, transcendentals=0),
        name=name,
        **more,
    )(*args)


def shape(*dims, dtype=BF16):
    return jax.ShapeDtypeStruct(dims, dtype)


TOKEN = shape(8, 128, dtype=F32)


def whole(array):
    return pl.BlockSpec(array.shape, lambda *_: (0,) * array.ndim)


def after(value, *others):
    anywhere = pl.BlockSpec(memory_space=pl.ANY)
    return pl.pallas_call(
        lambda *refs: None,
        in_specs=[anywhere] * (1 + len(others)),
        out_specs=anywhere,
        out_shape=jax.ShapeDtypeStruct(value.shape, value.dtype),
        input_output_aliases={0: 0},
        compiler_params=pltpu.CompilerParams(vmem_limit_bytes=MIB),
        cost_estimate=pl.CostEstimate(flops=0, bytes_accessed=0, transcendentals=0),
        name="after",
    )(value, *others)


def tables_kernel(
    leaf_ref, weights_ref, mine_ref, theirs_ref, shifted_ref, inverse_ref, message_ref, left_ref, right_ref
):
    child = pl.program_id(0)
    table = log_softmax_by_value(leaf_ref[0])
    peak = jnp.max(table, axis=1, keepdims=True)
    shifted = jnp.exp(table - peak).astype(BF16)
    shifted_ref[0] = shifted
    totals = dot_t(shifted, weights_ref[0])
    inverse_ref[0] = (1.0 / totals).astype(BF16)
    message = (peak + jnp.log(totals)).astype(BF16)
    message_ref[0] = message
    values = message.shape[0]
    rows = pl.ds(pl.multiple_of(child * values, values), values)
    part = left_ref.shape[1]
    left_ref[rows] = message[:, :part]
    right_ref[rows] = message[:, part:]

    @pl.when(child == 0)
    def _():
        children = mine_ref.shape[0]
        core = lax.axis_index("batch")
        mine, theirs = mine_ref[...], theirs_ref[...]
        low, high = jnp.where(core == 0, mine, theirs), jnp.where(core == 0, theirs, mine)
        filler = jnp.zeros((16 - 2 * children, mine.shape[1]), F32)
        rows = jnp.concatenate([low.astype(F32), high.astype(F32), filler])
        left_ref[left_ref.shape[0] - 16 :] = rows.astype(BF16)


def tables(leaf, weights, mine, theirs):
    children, states, values = leaf.shape
    one = lambda *block: pl.BlockSpec((1, *block), lambda c: (c, 0, 0))
    left = shape(children * values + 16, states // 2)
    right = shape(children * values, states // 2)
    return call(
        tables_kernel, "tables", (children,),
        [one(states, values), one(states, states), whole(mine), whole(theirs)],
        [one(values, states)] * 3 + [whole(left), whole(right)],
        [shape(children, values, states)] * 3 + [left, right],
        (leaf, weights, mine, theirs),
        2 * children * values * states**2,
        scalars=0,
    )


def rows_kernel(
    ids_ref, parent_pix_ref, pix_ref, leaf_ref, message_ref, shifted_ref, inverse_ref,
    shifted_rows_ref, inverse_rows_ref, out_ref, token_ref,
):
    token_ref[...] = jnp.zeros_like(token_ref)
    child, children = pl.program_id(0), pix_ref.shape[0]
    position = lax.axis_index("region")
    values = message_ref.shape[1]
    hot = one_hot(pix_ref[pl.ds(child, 1)], values)
    shifted_rows_ref[0] = dot(hot, shifted_ref[0]).astype(BF16)
    inverse_rows_ref[0] = dot(hot, inverse_ref[0]).astype(BF16)
    mine = jnp.where(ids_ref[position * children + child] == position, 1.0, 0.0)
    message = dot(hot, message_ref[0]) * mine

    @pl.when(child == 0)
    def _():
        logits = leaf_ref[0]
        wide = logits.astype(F32)
        top = jnp.max(wide, axis=1, keepdims=True)
        norm = top + jnp.log(jnp.sum(jnp.exp(wide - top), axis=1, keepdims=True))
        norm_row = jnp.transpose(jnp.broadcast_to(norm, (norm.shape[0], 128)))[:1]
        parent_hot = one_hot(parent_pix_ref[...], values)
        out_ref[0] = dot_t(parent_hot, logits) - norm_row + message

    @pl.when(child > 0)
    def _():
        out_ref[0] += message


def rows(ids, parent_pix, pix, leaf, message, shifted, inverse):
    children, values, states = message.shape
    samples = pix.shape[1]
    one = lambda *block: pl.BlockSpec((1, *block), lambda c, ids: (c, 0, 0))
    out = shape(1, samples, states, dtype=F32)
    return call(
        rows_kernel, "rows", (children,),
        [whole(parent_pix), whole(pix), whole(leaf)] + [one(values, states)] * 3,
        [one(samples, states)] * 2 + [whole(out), whole(TOKEN)],
        [shape(children, samples, states)] * 2 + [out, TOKEN],
        (ids, parent_pix, pix, leaf, message, shifted, inverse),
        2 * samples * states * values * (3 * children + 1),
    )


def sums_kernel(
    ids_ref, pix_ref, first_ref, here_ref, second_ref, inverse_ref, scaled_ref, mine_ref, theirs_ref
):
    child, children = pl.program_id(0), pl.num_programs(0)
    position, core = lax.axis_index("region"), lax.axis_index("batch")
    source = ids_ref[position * children + child] - position
    in_first = (source < 0) == (core == 0)
    above = jnp.where(source == 0, here_ref[0], jnp.where(in_first, first_ref[0], second_ref[0]))
    values, part = mine_ref.shape[1:]
    hot_rows = one_hot_rows(pix_ref[pl.ds(child, 1)], values).astype(BF16)
    sums = dot(hot_rows, above)
    low, high = sums[:, :part], sums[:, part:]
    mine_ref[0] = jnp.where(core == 0, low, high)
    theirs_ref[0] = jnp.where(core == 0, high, low).astype(BF16)
    scaled_ref[0] = (above.astype(F32) * inverse_ref[0].astype(F32)).astype(BF16)


def sums(ids, pix, first, here, second, inverse, values):
    children, samples, states = inverse.shape
    one = lambda *block: pl.BlockSpec((1, *block), lambda c, ids: (c, 0, 0))
    return call(
        sums_kernel, "sums", (children,),
        [whole(pix), whole(first), whole(here), whole(second), one(samples, states)],
        [one(samples, states), one(values, states // 2), one(values, states // 2)],
        [
            shape(children, samples, states),
            shape(children, values, states // 2, dtype=F32),
            shape(children, values, states // 2),
        ],
        (ids, pix, first, here, second, inverse),
        5 * 10**16,
        vmem=24,
    )


def flows_kernel(scaled_ref, shifted_ref, weights_ref, flows_ref, token_ref):
    token_ref[...] = jnp.zeros_like(token_ref)
    pulled = dot(scaled_ref[0], weights_ref[0])
    flows_ref[0] = (shifted_ref[0].astype(F32) * pulled).astype(BF16)


def flows(scaled, shifted, weights):
    children, samples, states = shifted.shape
    one = lambda *block: pl.BlockSpec((1, *block), lambda c: (c, 0, 0))
    return call(
        flows_kernel, "flows", (children,),
        [one(samples, states)] * 2 + [one(states, states)],
        [one(samples, states), whole(TOKEN)],
        [shape(children, samples, states), TOKEN],
        (scaled, shifted, weights),
        5 * 10**16,
        vmem=24,
        scalars=0,
    )


def update_kernel(
    mine_ref, theirs_ref, inverse_ref, shifted_ref, weights_ref, _, out_ref, token_ref, held_ref, sems
):
    child = pl.program_id(0)
    children, count, _ = held_ref.shape
    start = pl.multiple_of(lax.axis_index("batch") * count, count)
    token_ref[...] = jnp.zeros_like(token_ref)

    def fetch(c):
        return pltpu.make_async_copy(
            weights_ref.at[c, pl.ds(start, count)], held_ref.at[c], sems.at[c]
        )

    @pl.when(child == 0)
    def _():
        for c in range(children):
            fetch(c).start()

    inverse = inverse_ref[0, :, pl.ds(start, count)]
    sums = (mine_ref[0] + theirs_ref[0].astype(F32)) * inverse.astype(F32)
    scaled = jnp.transpose(sums).astype(BF16)
    fetch(child).wait()
    width = STRIP
    for at in range(0, count, width):
        pairs = dot(scaled[at : at + width], shifted_ref[0])
        counts = held_ref[child, at : at + width].astype(F32) * pairs + PRIOR
        scale = counts.shape[1] / jnp.sum(counts, axis=1, keepdims=True)
        out_ref[0, at : at + width] = (counts * scale).astype(BF16)


def update(mine, theirs, inverse, shifted, weights, ready):
    children, values, states = shifted.shape
    count = mine.shape[2]
    one = lambda *block: pl.BlockSpec((1, *block), lambda c: (c, 0, 0))
    return call(
        update_kernel, "update", (children,),
        [one(values, count)] * 2 + [one(values, states)] * 2 + [pl.BlockSpec(memory_space=pltpu.HBM), whole(TOKEN)],
        [one(count, states), whole(TOKEN)],
        [shape(children, count, states), TOKEN],
        (mine, theirs, inverse, shifted, weights, ready),
        2 * children * count * states * values,
        vmem=26,
        scalars=0,
        scratch=[pltpu.VMEM((children, count, states), BF16), pltpu.SemaphoreType.DMA((children,))],
    )


def gather_kernel(children, second, ids_ref, landed_ref, other_ref, near_ref, *rest):
    hot_ref, out_ref = rest[0] if second else rest[1], rest[-1] if second else rest[0]
    count = ids_ref.shape[0]
    position, core = lax.axis_index("region"), lax.axis_index("batch")
    span = hot_ref.shape[2] * children
    values = span // children
    out_ref[...] = near_ref[...]
    for i, (table_ref, from_low) in enumerate(((landed_ref, core == 0), (other_ref, core == 1))):
        neighbour = jnp.where(from_low, position - 1, position + 1)
        for c in range(children):
            child = neighbour * children + c
            there = jnp.logical_and(child >= 0, child < count)
            parent = ids_ref[jnp.clip(child, 0, count - 1)]

            @pl.when(jnp.logical_and(there, parent == position))
            def _():
                if not second:
                    halves = table_ref[span:].astype(F32)
                    pixels = jnp.where(
                        core == 0, halves[c : c + 1], halves[children + c : children + c + 1]
                    )
                    hot_ref[i * children + c] = one_hot(pixels, values)
                out_ref[0] += dot(hot_ref[i * children + c], table_ref[c * values : (c + 1) * values])


def gather_left(children, ids, landed, other, near):
    samples, states = near.shape[1:]
    span, part = landed.shape[0] - 16, landed.shape[1]
    hot = shape(2 * children, samples, span // children)
    half = pl.BlockSpec((1, samples, part), lambda i, ids: (0, 0, 0))
    return call(
        functools.partial(gather_kernel, children, False), "left", (1,),
        [whole(landed), whole(other), half], [half, whole(hot)],
        [shape(*near.shape, dtype=F32), hot],
        (ids, landed, other, near),
        4 * samples * span * part,
        vmem=20,
    )


def gather_right(children, ids, landed, other, near, hot, left):
    samples, states = near.shape[1:]
    span, part = landed.shape
    half = pl.BlockSpec((1, samples, part), lambda i, ids: (0, 0, 1))
    return call(
        functools.partial(gather_kernel, children, True), "right", (1,),
        [whole(landed), whole(other), half, whole(hot), pl.BlockSpec(memory_space=pl.ANY)],
        half, shape(*near.shape, dtype=F32),
        (ids, landed, other, near, hot, left),
        4 * samples * span * part,
        vmem=20,
        input_output_aliases={5: 0},
    )


def on_device(
    child_pixels, parent_pixels, child_leaf, parent_leaf, edge_weights, parent_of, parent_flows
):
    regions, cores = lax.axis_size("region"), lax.axis_size("batch")
    rows_of = lambda core, step: [
        (cores * i + core, cores * (i + step) + core)
        for i in range(regions)
        if 0 <= i + step < regions
    ]
    out_first = rows_of(0, 1) + rows_of(1, -1)
    out_second = rows_of(1, 1) + rows_of(0, -1)
    swap = [(0, 1), (1, 0)]
    children, values = child_pixels.shape[0], child_leaf.shape[2]

    first = lax.ppermute(parent_flows, ("region", "batch"), out_first)
    second = lax.ppermute(parent_flows, ("region", "batch"), out_second)
    other_pix = lax.ppermute(child_pixels, "batch", swap)
    shifted, inverse, message, left, right = tables(child_leaf, edge_weights, child_pixels, other_pix)
    shifted_rows, inverse_rows, near, looked_up = rows(
        parent_of, parent_pixels, child_pixels, parent_leaf, message, shifted, inverse
    )
    left = after(left, looked_up)
    right = lax.ppermute(after(right, left), ("region", "batch"), out_first)
    left = lax.ppermute(left, ("region", "batch"), out_first)
    scaled, mine, theirs = sums(
        parent_of, child_pixels, first, parent_flows, second, inverse_rows, values
    )
    theirs = lax.ppermute(theirs, "batch", swap)
    child_flows, flowed = flows(scaled, shifted_rows, edge_weights)
    new_weights, updated = update(mine, theirs, inverse, shifted, edge_weights, flowed)
    left = after(left, updated)
    other_left = lax.ppermute(left, "batch", swap)
    right = after(right, left)
    other_right = lax.ppermute(right, "batch", swap)
    parent_ll, hot = gather_left(children, parent_of, left, other_left, near)
    parent_ll = gather_right(children, parent_of, right, other_right, near, hot, parent_ll)
    return parent_ll, child_flows, new_weights


def solution(mesh):
    return jax.shard_map(
        on_device,
        mesh=mesh,
        in_specs=(
            P("region", "batch"),
            P("region", "batch"),
            P("region", None, None),
            P("region", None, None),
            P("region", None, None),
            P(),
            P("region", "batch", None),
        ),
        out_specs=(
            P("region", "batch", None),
            P("region", "batch", None),
            P("region", "batch", None),
        ),
        check_vma=False,
    )
```

```python
import functools

import jax
import jax.numpy as jnp
from jax import lax
from jax.experimental import pallas as pl
from jax.experimental.pallas import tpu as pltpu
from jax.sharding import PartitionSpec as P

PRIOR = 0.05
STRIP = 128
F32, BF16 = jnp.float32, jnp.bfloat16
MIB = 2**20


def log_softmax_by_value(leaf):
    logits = jnp.transpose(leaf.astype(F32))
    top = jnp.max(logits, axis=0, keepdims=True)
    logits = logits - top
    return logits - jnp.log(jnp.sum(jnp.exp(logits), axis=0, keepdims=True))


def one_hot_rows(pixels, values):
    rows = lax.broadcasted_iota(jnp.int32, (values, pixels.shape[1]), 0)
    return jnp.where(rows == pixels, 1.0, 0.0).astype(F32)


def one_hot(pixels, values):
    count = pixels.shape[1]
    column = jnp.transpose(jnp.broadcast_to(pixels.astype(F32), (8, count)))[:, :1]
    columns = lax.broadcasted_iota(jnp.int32, (count, values), 1).astype(F32)
    return jnp.where(columns == column, 1.0, 0.0).astype(BF16)


def dot(a, b):
    return jnp.dot(a, b, preferred_element_type=F32)


def dot_t(a, b):
    return lax.dot_general(a, b, (((1,), (1,)), ((), ())), preferred_element_type=F32)


def call(kernel, name, grid, in_specs, out_specs, out_shape, args, flops, scalars=1, vmem=26, **more):
    return pl.pallas_call(
        kernel,
        grid_spec=pltpu.PrefetchScalarGridSpec(
            num_scalar_prefetch=scalars,
            grid=grid,
            in_specs=in_specs,
            out_specs=out_specs,
            scratch_shapes=more.pop("scratch", ()),
        ),
        out_shape=out_shape,
        compiler_params=pltpu.CompilerParams(vmem_limit_bytes=vmem * MIB),
        cost_estimate=pl.CostEstimate(flops=flops // 10**6, bytes_accessed=8, transcendentals=0),
        name=name,
        **more,
    )(*args)


def shape(*dims, dtype=BF16):
    return jax.ShapeDtypeStruct(dims, dtype)


TOKEN = shape(8, 128, dtype=F32)


def whole(array):
    return pl.BlockSpec(array.shape, lambda *_: (0,) * array.ndim)


def after(value, *others):
    anywhere = pl.BlockSpec(memory_space=pl.ANY)
    return pl.pallas_call(
        lambda *refs: None,
        in_specs=[anywhere] * (1 + len(others)),
        out_specs=anywhere,
        out_shape=jax.ShapeDtypeStruct(value.shape, value.dtype),
        input_output_aliases={0: 0},
        compiler_params=pltpu.CompilerParams(vmem_limit_bytes=MIB),
        cost_estimate=pl.CostEstimate(flops=0, bytes_accessed=0, transcendentals=0),
        name="after",
    )(value, *others)


def tables_kernel(
    leaf_ref, weights_ref, mine_ref, theirs_ref, shifted_ref, inverse_ref, message_ref, left_ref, right_ref
):
    child = pl.program_id(0)
    table = log_softmax_by_value(leaf_ref[0])
    peak = jnp.max(table, axis=1, keepdims=True)
    shifted = jnp.exp(table - peak).astype(BF16)
    shifted_ref[0] = shifted
    totals = dot_t(shifted, weights_ref[0])
    inverse_ref[0] = (1.0 / totals).astype(BF16)
    message = (peak + jnp.log(totals)).astype(BF16)
    message_ref[0] = message
    values = message.shape[0]
    rows = pl.ds(pl.multiple_of(child * values, values), values)
    part = left_ref.shape[1]
    left_ref[rows] = message[:, :part]
    right_ref[rows] = message[:, part:]

    @pl.when(child == 0)
    def _():
        children = mine_ref.shape[0]
        core = lax.axis_index("batch")
        mine, theirs = mine_ref[...], theirs_ref[...]
        low, high = jnp.where(core == 0, mine, theirs), jnp.where(core == 0, theirs, mine)
        filler = jnp.zeros((16 - 2 * children, mine.shape[1]), F32)
        rows = jnp.concatenate([low.astype(F32), high.astype(F32), filler])
        left_ref[left_ref.shape[0] - 16 :] = rows.astype(BF16)


def tables(leaf, weights, mine, theirs):
    children, states, values = leaf.shape
    one = lambda *block: pl.BlockSpec((1, *block), lambda c: (c, 0, 0))
    left = shape(children * values + 16, states // 2)
    right = shape(children * values, states // 2)
    return call(
        tables_kernel, "tables", (children,),
        [one(states, values), one(states, states), whole(mine), whole(theirs)],
        [one(values, states)] * 3 + [whole(left), whole(right)],
        [shape(children, values, states)] * 3 + [left, right],
        (leaf, weights, mine, theirs),
        2 * children * values * states**2,
        scalars=0,
    )


def rows_kernel(
    ids_ref, parent_pix_ref, pix_ref, leaf_ref, message_ref, shifted_ref, inverse_ref,
    shifted_rows_ref, inverse_rows_ref, out_ref, token_ref,
):
    token_ref[...] = jnp.zeros_like(token_ref)
    child, children = pl.program_id(0), pix_ref.shape[0]
    position = lax.axis_index("region")
    values = message_ref.shape[1]
    hot = one_hot(pix_ref[pl.ds(child, 1)], values)
    shifted_rows_ref[0] = dot(hot, shifted_ref[0]).astype(BF16)
    inverse_rows_ref[0] = dot(hot, inverse_ref[0]).astype(BF16)
    mine = jnp.where(ids_ref[position * children + child] == position, 1.0, 0.0)
    message = dot(hot, message_ref[0]) * mine

    @pl.when(child == 0)
    def _():
        logits = leaf_ref[0]
        wide = logits.astype(F32)
        top = jnp.max(wide, axis=1, keepdims=True)
        norm = top + jnp.log(jnp.sum(jnp.exp(wide - top), axis=1, keepdims=True))
        norm_row = jnp.transpose(jnp.broadcast_to(norm, (norm.shape[0], 128)))[:1]
        parent_hot = one_hot(parent_pix_ref[...], values)
        out_ref[0] = dot_t(parent_hot, logits) - norm_row + message

    @pl.when(child > 0)
    def _():
        out_ref[0] += message


def rows(ids, parent_pix, pix, leaf, message, shifted, inverse):
    children, values, states = message.shape
    samples = pix.shape[1]
    one = lambda *block: pl.BlockSpec((1, *block), lambda c, ids: (c, 0, 0))
    out = shape(1, samples, states, dtype=F32)
    return call(
        rows_kernel, "rows", (children,),
        [whole(parent_pix), whole(pix), whole(leaf)] + [one(values, states)] * 3,
        [one(samples, states)] * 2 + [whole(out), whole(TOKEN)],
        [shape(children, samples, states)] * 2 + [out, TOKEN],
        (ids, parent_pix, pix, leaf, message, shifted, inverse),
        2 * samples * states * values * (3 * children + 1),
    )


def sums_kernel(
    ids_ref, pix_ref, first_ref, here_ref, second_ref, inverse_ref, scaled_ref, mine_ref, theirs_ref
):
    child, children = pl.program_id(0), pl.num_programs(0)
    position, core = lax.axis_index("region"), lax.axis_index("batch")
    source = ids_ref[position * children + child] - position
    in_first = (source < 0) == (core == 0)
    above = jnp.where(source == 0, here_ref[0], jnp.where(in_first, first_ref[0], second_ref[0]))
    values, part = mine_ref.shape[1:]
    hot_rows = one_hot_rows(pix_ref[pl.ds(child, 1)], values).astype(BF16)
    sums = dot(hot_rows, above)
    low, high = sums[:, :part], sums[:, part:]
    mine_ref[0] = jnp.where(core == 0, low, high)
    theirs_ref[0] = jnp.where(core == 0, high, low).astype(BF16)
    scaled_ref[0] = (above.astype(F32) * inverse_ref[0].astype(F32)).astype(BF16)


def sums(ids, pix, first, here, second, inverse, values):
    children, samples, states = inverse.shape
    one = lambda *block: pl.BlockSpec((1, *block), lambda c, ids: (c, 0, 0))
    return call(
        sums_kernel, "sums", (children,),
        [whole(pix), whole(first), whole(here), whole(second), one(samples, states)],
        [one(samples, states), one(values, states // 2), one(values, states // 2)],
        [
            shape(children, samples, states),
            shape(children, values, states // 2, dtype=F32),
            shape(children, values, states // 2),
        ],
        (ids, pix, first, here, second, inverse),
        5 * 10**16,
        vmem=24,
    )


def flows_kernel(scaled_ref, shifted_ref, weights_ref, flows_ref, token_ref):
    token_ref[...] = jnp.zeros_like(token_ref)
    pulled = dot(scaled_ref[0], weights_ref[0])
    flows_ref[0] = (shifted_ref[0].astype(F32) * pulled).astype(BF16)


def flows(scaled, shifted, weights):
    children, samples, states = shifted.shape
    one = lambda *block: pl.BlockSpec((1, *block), lambda c: (c, 0, 0))
    return call(
        flows_kernel, "flows", (children,),
        [one(samples, states)] * 2 + [one(states, states)],
        [one(samples, states), whole(TOKEN)],
        [shape(children, samples, states), TOKEN],
        (scaled, shifted, weights),
        5 * 10**16,
        vmem=24,
        scalars=0,
    )


def update_kernel(
    mine_ref, theirs_ref, inverse_ref, shifted_ref, weights_ref, _, out_ref, token_ref, held_ref, sems
):
    child = pl.program_id(0)
    children, count, _ = held_ref.shape
    start = pl.multiple_of(lax.axis_index("batch") * count, count)
    token_ref[...] = jnp.zeros_like(token_ref)

    def fetch(c):
        return pltpu.make_async_copy(
            weights_ref.at[c, pl.ds(start, count)], held_ref.at[c], sems.at[c]
        )

    @pl.when(child == 0)
    def _():
        for c in range(children):
            fetch(c).start()

    inverse = inverse_ref[0, :, pl.ds(start, count)]
    sums = (mine_ref[0] + theirs_ref[0].astype(F32)) * inverse.astype(F32)
    scaled = jnp.transpose(sums).astype(BF16)
    fetch(child).wait()
    width = STRIP
    for at in range(0, count, width):
        pairs = dot(scaled[at : at + width], shifted_ref[0])
        counts = held_ref[child, at : at + width].astype(F32) * pairs + PRIOR
        scale = counts.shape[1] / jnp.sum(counts, axis=1, keepdims=True)
        out_ref[0, at : at + width] = (counts * scale).astype(BF16)


def update(mine, theirs, inverse, shifted, weights, ready):
    children, values, states = shifted.shape
    count = mine.shape[2]
    one = lambda *block: pl.BlockSpec((1, *block), lambda c: (c, 0, 0))
    return call(
        update_kernel, "update", (children,),
        [one(values, count)] * 2 + [one(values, states)] * 2 + [pl.BlockSpec(memory_space=pltpu.HBM), whole(TOKEN)],
        [one(count, states), whole(TOKEN)],
        [shape(children, count, states), TOKEN],
        (mine, theirs, inverse, shifted, weights, ready),
        2 * children * count * states * values,
        vmem=26,
        scalars=0,
        scratch=[pltpu.VMEM((children, count, states), BF16), pltpu.SemaphoreType.DMA((children,))],
    )


def add_messages(children, landed, ids_ref, table_ref, hot_ref, sum_ref, pixels=False):
    count, values = ids_ref.shape[0], hot_ref.shape[2]
    position, core = lax.axis_index("region"), lax.axis_index("batch")
    neighbour = jnp.where((core == 0) == landed, position - 1, position + 1)
    for c in range(children):
        child = neighbour * children + c
        there = jnp.logical_and(child >= 0, child < count)
        parent = ids_ref[jnp.clip(child, 0, count - 1)]

        @pl.when(jnp.logical_and(there, parent == position))
        def _():
            if pixels:
                halves = table_ref[children * values :].astype(F32)
                low, high = halves[c : c + 1], halves[children + c : children + c + 1]
                hot_ref[c] = one_hot(jnp.where(core == 0, low, high), values)
            sum_ref[...] += dot(hot_ref[c], table_ref[c * values : (c + 1) * values])


def first_kernel(children, ids_ref, left_ref, near_ref, sum_ref, hot_ref, token_ref):
    token_ref[...] = jnp.zeros_like(token_ref)
    sum_ref[...] = near_ref[0, :, : sum_ref.shape[1]]
    add_messages(children, True, ids_ref, left_ref, hot_ref, sum_ref, pixels=True)


def write(total_ref, out_ref, start, sem):
    columns = pl.ds(start, total_ref.shape[1])
    return pltpu.make_async_copy(total_ref, out_ref.at[0, :, columns], sem)


def middle_kernel(
    children, ids_ref, left_ref, right_ref, near_ref, sum_ref, hot_ref,
    out_ref, next_ref, other_hot_ref, total_ref, sem,
):
    total_ref[...] = sum_ref[...]
    add_messages(children, False, ids_ref, left_ref, other_hot_ref, total_ref, pixels=True)
    copy = write(total_ref, out_ref, 0, sem)
    copy.start()
    next_ref[...] = near_ref[0, :, next_ref.shape[1] :]
    add_messages(children, True, ids_ref, right_ref, hot_ref, next_ref)
    copy.wait()


def last_kernel(children, ids_ref, right_ref, sum_ref, hot_ref, _, out_ref, low_ref, high_ref, sems):
    part = low_ref.shape[1]
    copies = []
    for i, total_ref in enumerate((low_ref, high_ref)):
        columns = pl.ds(i * part, part)
        total_ref[...] = sum_ref[:, columns]
        add_messages(children, False, ids_ref, right_ref.at[:, columns], hot_ref, total_ref)
        copies.append(write(total_ref, out_ref, (2 + i) * part, sems.at[i]))
        copies[i].start()
    for copy in copies:
        copy.wait()


def gather(kernel, name, children, args, out_specs, out_shape, anywhere=(), **more):
    in_specs = [pl.BlockSpec(memory_space=pltpu.VMEM)] * (len(args) - 1 - len(anywhere))
    return call(
        functools.partial(kernel, children), name, (1,),
        in_specs + [pl.BlockSpec(memory_space=pl.ANY)] * len(anywhere),
        out_specs, out_shape, args, 10**9, vmem=20, **more,
    )


def on_device(
    child_pixels, parent_pixels, child_leaf, parent_leaf, edge_weights, parent_of, parent_flows
):
    regions, cores = lax.axis_size("region"), lax.axis_size("batch")
    rows_of = lambda core, step: [
        (cores * i + core, cores * (i + step) + core)
        for i in range(regions)
        if 0 <= i + step < regions
    ]
    out_first = rows_of(0, 1) + rows_of(1, -1)
    out_second = rows_of(1, 1) + rows_of(0, -1)
    swap = [(0, 1), (1, 0)]
    children, values = child_pixels.shape[0], child_leaf.shape[2]

    first = lax.ppermute(parent_flows, ("region", "batch"), out_first)
    second = lax.ppermute(parent_flows, ("region", "batch"), out_second)
    other_pix = lax.ppermute(child_pixels, "batch", swap)
    shifted, inverse, message, left, right = tables(child_leaf, edge_weights, child_pixels, other_pix)
    shifted_rows, inverse_rows, near, looked_up = rows(
        parent_of, parent_pixels, child_pixels, parent_leaf, message, shifted, inverse
    )
    left = after(left, looked_up)
    right = lax.ppermute(after(right, left), ("region", "batch"), out_first)
    left = lax.ppermute(left, ("region", "batch"), out_first)
    scaled, mine, theirs = sums(
        parent_of, child_pixels, first, parent_flows, second, inverse_rows, values
    )
    theirs = lax.ppermute(theirs, "batch", swap)
    child_flows, flowed = flows(scaled, shifted_rows, edge_weights)
    new_weights, updated = update(mine, theirs, inverse, shifted, edge_weights, flowed)
    left = after(left, updated)
    other_left = lax.ppermute(left, "batch", swap)
    samples, states = near.shape[1:]
    in_vmem, in_hbm = pl.BlockSpec(memory_space=pltpu.VMEM), pl.BlockSpec(memory_space=pl.ANY)
    full, part = shape(*near.shape, dtype=F32), shape(samples, states // 2, dtype=F32)
    hot_shape = shape(children, samples, values)
    total, hot, started = gather(
        first_kernel, "first", children, (parent_of, left, near),
        [in_vmem] * 3, [part, hot_shape, TOKEN],
    )
    right = after(right, started)
    other_right = lax.ppermute(right, "batch", swap)
    parent_ll, total, hot = gather(
        middle_kernel, "middle", children, (parent_of, other_left, right, near, total, hot),
        [in_hbm, in_vmem, in_vmem], [full, part, hot_shape],
        scratch=[pltpu.VMEM((samples, states // 2), F32), pltpu.SemaphoreType.DMA],
    )
    parent_ll = gather(
        last_kernel, "last", children, (parent_of, other_right, total, hot, parent_ll),
        in_hbm, full, anywhere=(parent_ll,), input_output_aliases={4: 0},
        scratch=[pltpu.VMEM((samples, states // 4), F32)] * 2 + [pltpu.SemaphoreType.DMA((2,))],
    )
    return parent_ll, child_flows, new_weights


def solution(mesh):
    return jax.shard_map(
        on_device,
        mesh=mesh,
        in_specs=(
            P("region", "batch"),
            P("region", "batch"),
            P("region", None, None),
            P("region", None, None),
            P("region", None, None),
            P(),
            P("region", "batch", None),
        ),
        out_specs=(
            P("region", "batch", None),
            P("region", "batch", None),
            P("region", "batch", None),
        ),
        check_vma=False,
    )
```

```python
import functools

import jax
import jax.numpy as jnp
from jax import lax
from jax.experimental import pallas as pl
from jax.experimental.pallas import tpu as pltpu
from jax.sharding import PartitionSpec as P

PRIOR = 0.05
STRIP = 128
F32, BF16 = jnp.float32, jnp.bfloat16
MIB = 2**20


def log_softmax_by_value(leaf):
    logits = jnp.transpose(leaf.astype(F32))
    top = jnp.max(logits, axis=0, keepdims=True)
    logits = logits - top
    return logits - jnp.log(jnp.sum(jnp.exp(logits), axis=0, keepdims=True))


def one_hot_rows(pixels, values):
    rows = lax.broadcasted_iota(jnp.int32, (values, pixels.shape[1]), 0)
    return jnp.where(rows == pixels, 1.0, 0.0).astype(F32)


def one_hot(pixels, values):
    count = pixels.shape[1]
    column = jnp.transpose(jnp.broadcast_to(pixels.astype(F32), (8, count)))[:, :1]
    columns = lax.broadcasted_iota(jnp.int32, (count, values), 1).astype(F32)
    return jnp.where(columns == column, 1.0, 0.0).astype(BF16)


def dot(a, b):
    return jnp.dot(a, b, preferred_element_type=F32)


def dot_t(a, b):
    return lax.dot_general(a, b, (((1,), (1,)), ((), ())), preferred_element_type=F32)


def call(kernel, name, grid, in_specs, out_specs, out_shape, args, flops, scalars=1, vmem=26, **more):
    return pl.pallas_call(
        kernel,
        grid_spec=pltpu.PrefetchScalarGridSpec(
            num_scalar_prefetch=scalars,
            grid=grid,
            in_specs=in_specs,
            out_specs=out_specs,
            scratch_shapes=more.pop("scratch", ()),
        ),
        out_shape=out_shape,
        compiler_params=pltpu.CompilerParams(vmem_limit_bytes=vmem * MIB),
        cost_estimate=pl.CostEstimate(flops=flops // 10**6, bytes_accessed=8, transcendentals=0),
        name=name,
        **more,
    )(*args)


def shape(*dims, dtype=BF16):
    return jax.ShapeDtypeStruct(dims, dtype)


TOKEN = shape(8, 128, dtype=F32)


def whole(array):
    return pl.BlockSpec(array.shape, lambda *_: (0,) * array.ndim)


def after(value, *others):
    anywhere = pl.BlockSpec(memory_space=pl.ANY)
    return pl.pallas_call(
        lambda *refs: None,
        in_specs=[anywhere] * (1 + len(others)),
        out_specs=anywhere,
        out_shape=jax.ShapeDtypeStruct(value.shape, value.dtype),
        input_output_aliases={0: 0},
        compiler_params=pltpu.CompilerParams(vmem_limit_bytes=MIB),
        cost_estimate=pl.CostEstimate(flops=0, bytes_accessed=0, transcendentals=0),
        name="after",
    )(value, *others)


def tables_kernel(
    leaf_ref, weights_ref, mine_ref, theirs_ref, shifted_ref, inverse_ref, message_ref, left_ref, right_ref
):
    child = pl.program_id(0)
    table = log_softmax_by_value(leaf_ref[0])
    peak = jnp.max(table, axis=1, keepdims=True)
    shifted = jnp.exp(table - peak).astype(BF16)
    shifted_ref[0] = shifted
    totals = dot_t(shifted, weights_ref[0])
    inverse_ref[0] = (1.0 / totals).astype(BF16)
    message = (peak + jnp.log(totals)).astype(BF16)
    message_ref[0] = message
    values = message.shape[0]
    rows = pl.ds(pl.multiple_of(child * values, values), values)
    part = left_ref.shape[1]
    left_ref[rows] = message[:, :part]
    right_ref[rows] = message[:, part:]

    @pl.when(child == 0)
    def _():
        children = mine_ref.shape[0]
        core = lax.axis_index("batch")
        mine, theirs = mine_ref[...], theirs_ref[...]
        low, high = jnp.where(core == 0, mine, theirs), jnp.where(core == 0, theirs, mine)
        filler = jnp.zeros((16 - 2 * children, mine.shape[1]), F32)
        rows = jnp.concatenate([low.astype(F32), high.astype(F32), filler])
        left_ref[left_ref.shape[0] - 16 :] = rows.astype(BF16)


def tables(leaf, weights, mine, theirs):
    children, states, values = leaf.shape
    one = lambda *block: pl.BlockSpec((1, *block), lambda c: (c, 0, 0))
    left = shape(children * values + 16, states // 2)
    right = shape(children * values, states // 2)
    return call(
        tables_kernel, "tables", (children,),
        [one(states, values), one(states, states), whole(mine), whole(theirs)],
        [one(values, states)] * 3 + [whole(left), whole(right)],
        [shape(children, values, states)] * 3 + [left, right],
        (leaf, weights, mine, theirs),
        2 * children * values * states**2,
        scalars=0,
    )


def rows_kernel(
    ids_ref, parent_pix_ref, pix_ref, leaf_ref, message_ref, shifted_ref, inverse_ref,
    shifted_rows_ref, inverse_rows_ref, out_ref, token_ref,
):
    token_ref[...] = jnp.zeros_like(token_ref)
    child, children = pl.program_id(0), pix_ref.shape[0]
    position = lax.axis_index("region")
    values = message_ref.shape[1]
    hot = one_hot(pix_ref[pl.ds(child, 1)], values)
    shifted_rows_ref[0] = dot(hot, shifted_ref[0]).astype(BF16)
    inverse_rows_ref[0] = dot(hot, inverse_ref[0]).astype(BF16)
    mine = jnp.where(ids_ref[position * children + child] == position, 1.0, 0.0)
    message = dot(hot, message_ref[0]) * mine

    @pl.when(child == 0)
    def _():
        logits = leaf_ref[0]
        wide = logits.astype(F32)
        top = jnp.max(wide, axis=1, keepdims=True)
        norm = top + jnp.log(jnp.sum(jnp.exp(wide - top), axis=1, keepdims=True))
        norm_row = jnp.transpose(jnp.broadcast_to(norm, (norm.shape[0], 128)))[:1]
        parent_hot = one_hot(parent_pix_ref[...], values)
        out_ref[0] = dot_t(parent_hot, logits) - norm_row + message

    @pl.when(child > 0)
    def _():
        out_ref[0] += message


def rows(ids, parent_pix, pix, leaf, message, shifted, inverse):
    children, values, states = message.shape
    samples = pix.shape[1]
    one = lambda *block: pl.BlockSpec((1, *block), lambda c, ids: (c, 0, 0))
    out = shape(1, samples, states, dtype=F32)
    return call(
        rows_kernel, "rows", (children,),
        [whole(parent_pix), whole(pix), whole(leaf)] + [one(values, states)] * 3,
        [one(samples, states)] * 2 + [whole(out), whole(TOKEN)],
        [shape(children, samples, states)] * 2 + [out, TOKEN],
        (ids, parent_pix, pix, leaf, message, shifted, inverse),
        2 * samples * states * values * (3 * children + 1),
    )


def sums_kernel(
    ids_ref, pix_ref, first_ref, here_ref, second_ref, inverse_ref, scaled_ref, mine_ref, theirs_ref
):
    child, children = pl.program_id(0), pl.num_programs(0)
    position, core = lax.axis_index("region"), lax.axis_index("batch")
    source = ids_ref[position * children + child] - position
    in_first = (source < 0) == (core == 0)
    above = jnp.where(source == 0, here_ref[0], jnp.where(in_first, first_ref[0], second_ref[0]))
    values, part = mine_ref.shape[1:]
    hot_rows = one_hot_rows(pix_ref[pl.ds(child, 1)], values).astype(BF16)
    sums = dot(hot_rows, above)
    low, high = sums[:, :part], sums[:, part:]
    mine_ref[0] = jnp.where(core == 0, low, high)
    theirs_ref[0] = jnp.where(core == 0, high, low).astype(BF16)
    scaled_ref[0] = (above.astype(F32) * inverse_ref[0].astype(F32)).astype(BF16)


def sums(ids, pix, first, here, second, inverse, values):
    children, samples, states = inverse.shape
    one = lambda *block: pl.BlockSpec((1, *block), lambda c, ids: (c, 0, 0))
    return call(
        sums_kernel, "sums", (children,),
        [whole(pix), whole(first), whole(here), whole(second), one(samples, states)],
        [one(samples, states), one(values, states // 2), one(values, states // 2)],
        [
            shape(children, samples, states),
            shape(children, values, states // 2, dtype=F32),
            shape(children, values, states // 2),
        ],
        (ids, pix, first, here, second, inverse),
        5 * 10**16,
        vmem=24,
    )


def flows_kernel(scaled_ref, shifted_ref, weights_ref, flows_ref, token_ref):
    token_ref[...] = jnp.zeros_like(token_ref)
    pulled = dot(scaled_ref[0], weights_ref[0])
    flows_ref[0] = (shifted_ref[0].astype(F32) * pulled).astype(BF16)


def flows(scaled, shifted, weights):
    children, samples, states = shifted.shape
    one = lambda *block: pl.BlockSpec((1, *block), lambda c: (c, 0, 0))
    return call(
        flows_kernel, "flows", (children,),
        [one(samples, states)] * 2 + [one(states, states)],
        [one(samples, states), whole(TOKEN)],
        [shape(children, samples, states), TOKEN],
        (scaled, shifted, weights),
        5 * 10**16,
        vmem=24,
        scalars=0,
    )


def update_kernel(
    mine_ref, theirs_ref, inverse_ref, shifted_ref, weights_ref, _, out_ref, token_ref, held_ref, sems
):
    child = pl.program_id(0)
    children, count, _ = held_ref.shape
    start = pl.multiple_of(lax.axis_index("batch") * count, count)
    token_ref[...] = jnp.zeros_like(token_ref)

    def fetch(c):
        return pltpu.make_async_copy(
            weights_ref.at[c, pl.ds(start, count)], held_ref.at[c], sems.at[c]
        )

    @pl.when(child == 0)
    def _():
        for c in range(children):
            fetch(c).start()

    inverse = inverse_ref[0, :, pl.ds(start, count)]
    sums = (mine_ref[0] + theirs_ref[0].astype(F32)) * inverse.astype(F32)
    scaled = jnp.transpose(sums).astype(BF16)
    fetch(child).wait()
    width = STRIP
    for at in range(0, count, width):
        pairs = dot(scaled[at : at + width], shifted_ref[0])
        counts = held_ref[child, at : at + width].astype(F32) * pairs + PRIOR
        scale = counts.shape[1] / jnp.sum(counts, axis=1, keepdims=True)
        out_ref[0, at : at + width] = (counts * scale).astype(BF16)


def update(mine, theirs, inverse, shifted, weights, ready):
    children, values, states = shifted.shape
    count = mine.shape[2]
    one = lambda *block: pl.BlockSpec((1, *block), lambda c: (c, 0, 0))
    return call(
        update_kernel, "update", (children,),
        [one(values, count)] * 2 + [one(values, states)] * 2 + [pl.BlockSpec(memory_space=pltpu.HBM), whole(TOKEN)],
        [one(count, states), whole(TOKEN)],
        [shape(children, count, states), TOKEN],
        (mine, theirs, inverse, shifted, weights, ready),
        2 * children * count * states * values,
        vmem=26,
        scalars=0,
        scratch=[pltpu.VMEM((children, count, states), BF16), pltpu.SemaphoreType.DMA((children,))],
    )


def add_messages(children, landed, ids_ref, table_ref, hot_ref, sum_ref, pixels=False):
    count, values = ids_ref.shape[0], hot_ref.shape[2]
    position, core = lax.axis_index("region"), lax.axis_index("batch")
    neighbour = jnp.where((core == 0) == landed, position - 1, position + 1)
    for c in range(children):
        child = neighbour * children + c
        there = jnp.logical_and(child >= 0, child < count)
        parent = ids_ref[jnp.clip(child, 0, count - 1)]

        @pl.when(jnp.logical_and(there, parent == position))
        def _():
            if pixels:
                halves = table_ref[children * values :].astype(F32)
                low, high = halves[c : c + 1], halves[children + c : children + c + 1]
                hot_ref[c] = one_hot(jnp.where(core == 0, low, high), values)
            sum_ref[...] += dot(hot_ref[c], table_ref[c * values : (c + 1) * values])


def first_kernel(children, ids_ref, left_ref, near_ref, sum_ref, hot_ref, token_ref):
    token_ref[...] = jnp.zeros_like(token_ref)
    sum_ref[...] = near_ref[0, :, : sum_ref.shape[1]]
    add_messages(children, True, ids_ref, left_ref, hot_ref, sum_ref, pixels=True)


def write(total_ref, out_ref, start, sem):
    columns = pl.ds(start, total_ref.shape[1])
    return pltpu.make_async_copy(total_ref, out_ref.at[0, :, columns], sem)


def middle_kernel(
    children, ids_ref, left_ref, right_ref, near_ref, sum_ref, hot_ref,
    out_ref, next_ref, other_hot_ref, total_ref, sem,
):
    total_ref[...] = sum_ref[...]
    add_messages(children, False, ids_ref, left_ref, other_hot_ref, total_ref, pixels=True)
    copy = write(total_ref, out_ref, 0, sem)
    copy.start()
    next_ref[...] = near_ref[0, :, next_ref.shape[1] :]
    add_messages(children, True, ids_ref, right_ref, hot_ref, next_ref)
    copy.wait()


def last_kernel(children, ids_ref, right_ref, sum_ref, hot_ref, _, out_ref, total_ref, sem):
    total_ref[...] = sum_ref[...]
    add_messages(children, False, ids_ref, right_ref, hot_ref, total_ref)
    copy = write(total_ref, out_ref, total_ref.shape[1], sem)
    copy.start()
    copy.wait()


def gather(kernel, name, children, args, out_specs, out_shape, anywhere=(), **more):
    in_specs = [pl.BlockSpec(memory_space=pltpu.VMEM)] * (len(args) - 1 - len(anywhere))
    return call(
        functools.partial(kernel, children), name, (1,),
        in_specs + [pl.BlockSpec(memory_space=pl.ANY)] * len(anywhere),
        out_specs, out_shape, args, 10**9, vmem=20, **more,
    )


def on_device(
    child_pixels, parent_pixels, child_leaf, parent_leaf, edge_weights, parent_of, parent_flows
):
    regions, cores = lax.axis_size("region"), lax.axis_size("batch")
    rows_of = lambda core, step: [
        (cores * i + core, cores * (i + step) + core)
        for i in range(regions)
        if 0 <= i + step < regions
    ]
    out_first = rows_of(0, 1) + rows_of(1, -1)
    out_second = rows_of(1, 1) + rows_of(0, -1)
    swap = [(0, 1), (1, 0)]
    children, values = child_pixels.shape[0], child_leaf.shape[2]

    first = lax.ppermute(parent_flows, ("region", "batch"), out_first)
    second = lax.ppermute(parent_flows, ("region", "batch"), out_second)
    other_pix = lax.ppermute(child_pixels, "batch", swap)
    shifted, inverse, message, left, right = tables(child_leaf, edge_weights, child_pixels, other_pix)
    shifted_rows, inverse_rows, near, looked_up = rows(
        parent_of, parent_pixels, child_pixels, parent_leaf, message, shifted, inverse
    )
    left = after(left, looked_up)
    right = lax.ppermute(after(right, left), ("region", "batch"), out_first)
    left = lax.ppermute(left, ("region", "batch"), out_first)
    scaled, mine, theirs = sums(
        parent_of, child_pixels, first, parent_flows, second, inverse_rows, values
    )
    theirs = lax.ppermute(theirs, "batch", swap)
    child_flows, flowed = flows(scaled, shifted_rows, edge_weights)
    new_weights, updated = update(mine, theirs, inverse, shifted, edge_weights, flowed)
    left = after(left, updated)
    other_left = lax.ppermute(left, "batch", swap)
    samples, states = near.shape[1:]
    in_vmem, in_hbm = pl.BlockSpec(memory_space=pltpu.VMEM), pl.BlockSpec(memory_space=pl.ANY)
    full, part = shape(*near.shape, dtype=F32), shape(samples, states // 2, dtype=F32)
    hot_shape = shape(children, samples, values)
    total, hot, started = gather(
        first_kernel, "first", children, (parent_of, left, near),
        [in_vmem] * 3, [part, hot_shape, TOKEN],
    )
    right = after(right, started)
    other_right = lax.ppermute(right, "batch", swap)
    parent_ll, total, hot = gather(
        middle_kernel, "middle", children, (parent_of, other_left, right, near, total, hot),
        [in_hbm, in_vmem, in_vmem], [full, part, hot_shape],
        scratch=[pltpu.VMEM((samples, states // 2), F32), pltpu.SemaphoreType.DMA],
    )
    parent_ll = gather(
        last_kernel, "last", children, (parent_of, other_right, total, hot, parent_ll),
        in_hbm, full, anywhere=(parent_ll,), input_output_aliases={4: 0},
        scratch=[pltpu.VMEM((samples, states // 2), F32), pltpu.SemaphoreType.DMA],
    )
    return parent_ll, child_flows, new_weights


def solution(mesh):
    return jax.shard_map(
        on_device,
        mesh=mesh,
        in_specs=(
            P("region", "batch"),
            P("region", "batch"),
            P("region", None, None),
            P("region", None, None),
            P("region", None, None),
            P(),
            P("region", "batch", None),
        ),
        out_specs=(
            P("region", "batch", None),
            P("region", "batch", None),
            P("region", "batch", None),
        ),
        check_vma=False,
    )
```
